256 devices in a mesh: seq: 16 (over z_hi, y, core), res: 16 (over z_lo, x).
Axes of the slice: x: 4, y: 4, z: 8 (z_hi: 2, z_lo: 4; z = z_hi * 4 + z_lo), core: 2. Of those that a mesh axis runs over, the one named last changes fastest.
Arguments:
- alignment_embedding: bfloat16 [128, 2048, 256], P('seq', 'res'), may hold values from -6 to 6
- coupling_embedding: bfloat16 [2048, 2048, 128], P('res', 'seq'), may hold values from -6 to 6
- asking_projection: bfloat16 [256, 256], replicated, may hold values from -0.5 to 0.5
- lookup_projection: bfloat16 [256, 256], replicated, may hold values from -0.5 to 0.5
- content_projection: bfloat16 [256, 256], replicated, may hold values from -0.375 to 0.375
- filter_projection: bfloat16 [256, 256], replicated, may hold values from -0.375 to 0.375
- filter_offset: float32 [256], replicated, may hold values from -4 to 4
- coupling_head_projection: bfloat16 [128, 8], replicated, may hold values from -30 to 30, as said below
- final_projection: bfloat16 [256, 256], replicated, may hold values from -1.796875 to 1.796875
- final_offset: float32 [256], replicated, may hold values from -1.8 to 1.8
Outputs:
- update: bfloat16 [128, 2048, 256], P('seq', 'res')
The draws below stay inside these ranges and needn't reach their ends.
Inputs may be any that keep to these rules, and one draw needn't show every extreme that they name: `coupling_head_projection`: a real matrix of head biases.
All inputs are finite; a program needn't handle non-finite values.
Results may differ from the reference program's by a relative error of at most 0.0065.
The reference program's roundings to bfloat16 on the way count: a program that leaves them out, or rounds other values in their place, can miss the bound.
Values may be sent and summed in bfloat16 or wider, within the bound.
A program may use at most 128 MiB of HBM per device.

```python
import jax
import jax.numpy as jnp
from jax import lax

ALIGNMENT_DEPTH = 256
H = 8
DH = 32
CZ = 128
ALIGNED_STRANDS = 128
AMINO_TOTAL = 2048


def draw_coupling_head_projection(key, part):
    key = jax.random.fold_in(key, 7)
    base_key = jax.random.fold_in(key, 0)
    base = jnp.clip(jax.random.normal(base_key, (CZ, H), jnp.float32), -4.0, 4.0) / CZ ** 0.5
    return base.astype(jnp.bfloat16)


def block_levels(own_key, shape, shards, smallest, high):
    loudness, own = 1.0, jax.random.fold_in(own_key, 6)
    for axis_at, blocks in shards:
        steps = jnp.exp(jax.random.uniform(jax.random.fold_in(own, axis_at), (blocks,), jnp.float32, smallest / len(shards), high / len(shards)))
        loudness = loudness * jnp.repeat(steps, shape[axis_at] // blocks).reshape([-1 if axis == axis_at else 1 for axis in range(len(shape))])
    return loudness


def normal_values(key, extent, scale, reach, cuts=(), kind=jnp.bfloat16):
    values = jax.random.normal(key, extent, jnp.float32) * scale
    if len(cuts) > 0:
        values = block_levels(key, extent, cuts, -0.22, 0.18) * values
    return jnp.clip(values, min=-reach, max=reach).astype(kind)


def setup_inputs(seed: int = 0) -> dict:
    arg_keys = jax.random.split(jax.random.key(seed), 11)
    return {
        "alignment_embedding": normal_values(arg_keys[0], (ALIGNED_STRANDS, AMINO_TOTAL, ALIGNMENT_DEPTH), 1.0, 6.0, ((0, 16), (1, 16))),
        "coupling_embedding": normal_values(arg_keys[1], (AMINO_TOTAL, AMINO_TOTAL, CZ), 1.0, 6.0, ((0, 16), (1, 16))),
        "asking_projection": normal_values(arg_keys[2], (ALIGNMENT_DEPTH, ALIGNMENT_DEPTH), (ALIGNMENT_DEPTH // 2) ** -0.5, 0.5),
        "lookup_projection": normal_values(arg_keys[3], (ALIGNMENT_DEPTH, ALIGNMENT_DEPTH), (ALIGNMENT_DEPTH // 2) ** -0.5, 0.5),
        "content_projection": normal_values(arg_keys[4], (ALIGNMENT_DEPTH, ALIGNMENT_DEPTH), ALIGNMENT_DEPTH ** -0.5, 0.375),
        "filter_projection": normal_values(arg_keys[5], (ALIGNMENT_DEPTH, ALIGNMENT_DEPTH), ALIGNMENT_DEPTH ** -0.5, 0.375),
        "filter_offset": normal_values(arg_keys[6], (ALIGNMENT_DEPTH,), 1.0, 4.0, (), jnp.float32),
        "coupling_head_projection": draw_coupling_head_projection(jax.random.fold_in(arg_keys[10], 71), 0),
        "final_projection": normal_values(arg_keys[8], (ALIGNMENT_DEPTH, ALIGNMENT_DEPTH), 0.3, 1.796875),
        "final_offset": normal_values(arg_keys[9], (ALIGNMENT_DEPTH,), 0.3, 1.8, (), jnp.float32),
    }


def standardize_features(x):
    x = x.astype(jnp.float32)
    mean = lax.optimization_barrier(jnp.mean(x, axis=-1, keepdims=True))
    var = lax.optimization_barrier(jnp.mean((x - mean) ** 2, axis=-1, keepdims=True))
    return (x - mean) / jnp.sqrt(var + 1e-05)

def reference(alignment_embedding, coupling_embedding, asking_projection, lookup_projection, content_projection, filter_projection, filter_offset, coupling_head_projection, final_projection, final_offset):
    pair_normed = standardize_features(coupling_embedding).astype(jnp.bfloat16)
    bias = jnp.einsum('ijc,ch->hij', pair_normed.astype(jnp.float32), coupling_head_projection.astype(jnp.float32)).astype(jnp.bfloat16)
    bias_f = bias.astype(jnp.float32)
    scale = 1.0 / DH ** 0.5

    def lone_strand(row):
        standardized_embedding = standardize_features(row).astype(jnp.bfloat16)
        query = (jnp.dot(standardized_embedding, asking_projection, preferred_element_type=jnp.float32) * scale).astype(jnp.bfloat16)
        key = jnp.dot(standardized_embedding, lookup_projection, preferred_element_type=jnp.float32).astype(jnp.bfloat16)
        value = jnp.dot(standardized_embedding, content_projection, preferred_element_type=jnp.float32).astype(jnp.bfloat16)
        sigmoid_filter = jax.nn.sigmoid(jnp.dot(standardized_embedding, filter_projection, preferred_element_type=jnp.float32) + filter_offset)
        qh = query.reshape(AMINO_TOTAL, H, DH).astype(jnp.float32)
        kh = key.reshape(AMINO_TOTAL, H, DH).astype(jnp.float32)
        vh = value.reshape(AMINO_TOTAL, H, DH).astype(jnp.float32)
        scores = jnp.einsum('qhd,khd->hqk', qh, kh) + bias_f
        top = lax.optimization_barrier(jnp.max(scores, axis=-1, keepdims=True))
        weights = jnp.exp(scores - top)
        total = lax.optimization_barrier(jnp.sum(weights, axis=-1))
        wb = weights.astype(jnp.bfloat16).astype(jnp.float32)
        mixed_features = jnp.einsum('hqk,khd->qhd', wb, vh) / jnp.transpose(total)[:, :, None]
        filtered_update = (sigmoid_filter * mixed_features.reshape(AMINO_TOTAL, ALIGNMENT_DEPTH)).astype(jnp.bfloat16)
        return (jnp.dot(filtered_update, final_projection, preferred_element_type=jnp.float32) + final_offset).astype(jnp.bfloat16)
    return lax.map(lone_strand, alignment_embedding)
```

```python
import functools
import math

import jax
import jax.numpy as jnp
from jax import lax
from jax.experimental import pallas as pl
from jax.experimental.pallas import tpu as pltpu
from jax.sharding import PartitionSpec as P

MESH = pl.DeviceIdType.MESH
VMEM_LIMIT = 60 * 1024 * 1024
HEAD_GROUPS = 4


def standardize_features(x):
    x = x.astype(jnp.float32)
    mean = jnp.mean(x, axis=-1, keepdims=True)
    var = jnp.mean((x - mean) ** 2, axis=-1, keepdims=True)
    return (x - mean) * lax.rsqrt(var + 1e-05)


def bias_tile_kernel(pair_ref, w_ref, out_ref, scratch):
    step = pl.program_id(0)
    block = pair_ref.shape[0]
    queries = out_ref.shape[2]
    heads = w_ref.shape[0]
    normed = standardize_features(pair_ref[...]).astype(jnp.bfloat16)
    w = w_ref[...]
    for i in range(block):
        tile = lax.dot_general(w, normed[i], (((1,), (1,)), ((), ())), preferred_element_type=jnp.float32)
        scratch[pl.ds(pl.multiple_of((step * block + i) * heads, heads), heads), :] = tile

    @pl.when(step == pl.num_programs(0) - 1)
    def _():
        for h in range(heads):
            tile = scratch[pl.ds(h, queries, stride=heads), :]
            out_ref[h] = tile.T.astype(jnp.bfloat16)


def bias_tile(pair, w_t):
    queries, keys, depth = pair.shape
    heads = w_t.shape[0]
    block = 16
    return pl.pallas_call(
        bias_tile_kernel,
        grid=(queries // block,),
        out_shape=jax.ShapeDtypeStruct((heads, keys, queries), jnp.bfloat16),
        in_specs=[
            pl.BlockSpec((block, keys, depth), lambda i: (i, 0, 0)),
            pl.BlockSpec((heads, depth), lambda i: (0, 0)),
        ],
        out_specs=pl.BlockSpec((heads, keys, queries), lambda i: (0, 0, 0)),
        scratch_shapes=[pltpu.VMEM((queries * heads, keys), jnp.float32)],
        compiler_params=pltpu.CompilerParams(vmem_limit_bytes=VMEM_LIMIT),
    )(pair, w_t)


def coordinates():
    s, r = lax.axis_index("seq"), lax.axis_index("res")
    return s % 2, (s // 2) % 4, s // 8, r % 4, r // 4


def exchange_kernel(
    n_ref, t_ref, nall_ref, ball_ref, lsem, zs, zr, xs, xr, bs, br, ys, yr, cs, cr
):
    c, y, zh, x, zl = coordinates()
    qh = zl // 2
    half = n_ref.shape[0] // 2
    groups = bs.shape[1]
    per = t_ref.shape[0] // groups

    def device(c_=c, y_=y, zh_=zh, x_=x, zl_=zl):
        return (zh_ * 8 + y_ * 2 + c_, zl_ * 4 + x_)

    z_peers = [device(zl_=(zl + d) % 4) for d in (1, 2, 3)]
    x_peers = [device(x_=(x + d) % 4) for d in (1, 2, 3)]
    y_peers = [device(y_=(y + d) % 4) for d in (1, 2, 3)]
    b_peers = [
        device(zl_=(zl + 2) % 4),
        device(zh_=1 - zh),
        device(zh_=1 - zh, zl_=(zl + 2) % 4),
    ]
    sibling = device(c_=1 - c)
    peers = z_peers + x_peers + y_peers + b_peers[1:] + [sibling]

    own_n = pltpu.make_async_copy(n_ref.at[pl.ds(qh * half, half)], nall_ref.at[:, x, zl], lsem.at[0])
    own_b = pltpu.make_async_copy(t_ref, ball_ref.at[:, c, y, zh, qh], lsem.at[1])
    own_n.start()
    own_b.start()

    barrier = pltpu.get_barrier_semaphore()
    for peer in peers:
        pl.semaphore_signal(barrier, inc=1, device_id=peer, device_id_type=MESH)
    pl.semaphore_wait(barrier, len(peers))

    def remote(src, dst, send, recv, peer):
        return pltpu.make_async_remote_copy(
            src_ref=src, dst_ref=dst, send_sem=send, recv_sem=recv, device_id=peer, device_id_type=MESH
        )

    def z_copy(k, d):
        to = (zl + d + 1) % 4
        return remote(
            n_ref.at[(to // 2) * half + k], nall_ref.at[k, x, zl], zs.at[k, d], zr.at[k, d], z_peers[d]
        )

    def x_copy(k, d):
        return remote(nall_ref.at[k, x], nall_ref.at[k, x], xs.at[k, d], xr.at[k, d], x_peers[d])

    def b_copy(g, d):
        at = pl.ds(g * per, per)
        return remote(
            t_ref.at[at], ball_ref.at[at, c, y, zh, qh], bs.at[d, g], br.at[d, g], b_peers[d]
        )

    def y_copy(g, d):
        at = pl.ds(g * per, per)
        return remote(ball_ref.at[at, c, y], ball_ref.at[at, c, y], ys.at[d, g], yr.at[d, g], y_peers[d])

    def c_copy(g):
        at = pl.ds(g * per, per)
        return remote(ball_ref.at[at, c], ball_ref.at[at, c], cs.at[g], cr.at[g], sibling)

    three = range(3)
    for k in range(max(half, groups)):
        if k < groups:
            for d in three:
                b_copy(k, d).start()
        if k < half:
            for d in three:
                z_copy(k, d).start()
    own_n.wait()
    own_b.wait()
    for k in range(max(half, groups)):
        if k < groups:
            for d in three:
                b_copy(k, d).wait_recv()
            for d in three:
                y_copy(k, d).start()
        if k < half:
            for d in three:
                z_copy(k, d).wait_recv()
            for d in three:
                x_copy(k, d).start()
    for g in range(groups):
        for d in three:
            y_copy(g, d).wait_recv()
        c_copy(g).start()
    for k in range(half):
        for d in three:
            x_copy(k, d).wait_recv()
    for g in range(groups):
        c_copy(g).wait_recv()
    for k in range(half):
        for d in three:
            z_copy(k, d).wait_send()
            x_copy(k, d).wait_send()
    for g in range(groups):
        for d in three:
            b_copy(g, d).wait_send()
            y_copy(g, d).wait_send()
        c_copy(g).wait_send()


def exchange(normed, tile):
    rows, block, depth = normed.shape
    heads = tile.shape[0]
    half = rows // 2
    sem = pltpu.SemaphoreType.DMA
    return pl.pallas_call(
        exchange_kernel,
        out_shape=(
            jax.ShapeDtypeStruct((half, 4, 4, block, depth), jnp.bfloat16),
            jax.ShapeDtypeStruct((heads, 2, 4, 2, 2, block, block), jnp.bfloat16),
        ),
        in_specs=[pl.BlockSpec(memory_space=pl.ANY)] * 2,
        out_specs=(pl.BlockSpec(memory_space=pl.ANY),) * 2,
        scratch_shapes=[
            sem((2,)),
            sem((half, 3)),
            sem((half, 3)),
            sem((half, 3)),
            sem((half, 3)),
            sem((3, HEAD_GROUPS)),
            sem((3, HEAD_GROUPS)),
            sem((3, HEAD_GROUPS)),
            sem((3, HEAD_GROUPS)),
            sem((HEAD_GROUPS,)),
            sem((HEAD_GROUPS,)),
        ],
        compiler_params=pltpu.CompilerParams(collective_id=0, has_side_effects=True),
    )(normed, tile)


NT = (((1,), (1,)), ((), ()))


def attention_kernel(
    n_ref, b_ref, wq_ref, wk_ref, wv_ref, wf_ref, off_ref, wo_ref, oo_ref,
    out_ref, k_scr, v_scr, q_scr, g_scr, a_scr, s_scr,
):
    h, r = pl.program_id(0), pl.program_id(1)
    heads = pl.num_programs(0)
    depth = wq_ref.shape[0]
    size = depth // 8
    keys = n_ref.shape[1]
    block = 128
    scale = 1.0 / size**0.5

    @pl.when(h == 0)
    def _():
        _, _, _, x, zl = coordinates()
        first = pl.multiple_of((x * 4 + zl % 2) * block, block)
        second = pl.multiple_of((x * 4 + zl % 2 + 2) * block, block)
        rows_q = jnp.concatenate([n_ref[r, pl.ds(first, block), :], n_ref[r, pl.ds(second, block), :]], axis=0)
        q = lax.dot_general(wq_ref[...], rows_q, NT, preferred_element_type=jnp.float32) * scale
        q_scr[r] = q.astype(jnp.bfloat16)
        gate = lax.dot_general(wf_ref[...], rows_q, NT, preferred_element_type=jnp.float32) + off_ref[...]
        g_scr[r] = jax.nn.sigmoid(gate)
        for at in range(0, keys, 512):
            part = n_ref[r, pl.ds(at, 512), :]
            k_scr[r, pl.ds(at, 512), :] = jnp.dot(part, wk_ref[...], preferred_element_type=jnp.float32).astype(jnp.bfloat16)
            v = lax.dot_general(wv_ref[...], part, NT, preferred_element_type=jnp.float32).astype(jnp.bfloat16)
            for hh in range(8):
                v_scr[r, hh, pl.ds(0, size), pl.ds(at, 512)] = v[hh * size:(hh + 1) * size]
                v_scr[r, hh, pl.ds(size, 16), pl.ds(at, 512)] = jnp.ones((16, 512), jnp.bfloat16)

    qt = q_scr[r]
    channel = lax.broadcasted_iota(jnp.int32, qt.shape, 0)
    qm = jnp.where(channel // size == h, qt, jnp.zeros_like(qt))
    top = None
    step = 256
    for at in range(0, keys, step):
        s = jnp.dot(k_scr[r, pl.ds(at, step), :], qm, preferred_element_type=jnp.float32)
        parts = []
        for sub in range(at // block, (at + step) // block):
            j = (sub % 4) * 4 + sub // 4
            at_j = (0, j % 2, (j // 2) % 4, j // 8)
            parts.append(jnp.concatenate([b_ref[at_j + (0,)], b_ref[at_j + (1,)]], axis=1))
        s = s + jnp.concatenate(parts, axis=0).astype(jnp.float32)
        s_scr[pl.ds(at, step), :] = s
        best = jnp.max(s, axis=0, keepdims=True)
        top = best if top is None else jnp.maximum(top, best)
    acc = None
    for at in range(0, keys, step):
        w = jnp.exp(s_scr[pl.ds(at, step), :] - top).astype(jnp.bfloat16)
        part = jnp.dot(v_scr[r, h, :, pl.ds(at, step)], w, preferred_element_type=jnp.float32)
        acc = part if acc is None else acc + part
    a_scr[r, pl.ds(pl.multiple_of(h * size, size), size), :] = acc[:size] / acc[size:size + 1]

    @pl.when(h == heads - 1)
    def _():
        gated = (g_scr[r] * a_scr[r]).T.astype(jnp.bfloat16)
        out = jnp.dot(gated, wo_ref[...], preferred_element_type=jnp.float32) + oo_ref[...]
        out_ref[r] = out.astype(jnp.bfloat16)


def attention(nall, ball, wq, wk, wv, wf, off, wo, oo):
    rows, _, _, block, depth = nall.shape
    keys = 16 * block
    heads = ball.shape[0]
    size = depth // heads
    whole = lambda a: pl.BlockSpec(a.shape, lambda h, r: (0,) * a.ndim)
    n = nall.reshape(rows, keys, depth)
    weights = (wq.T, wk, wv.T, wf.T, off.reshape(depth, 1), wo, oo.reshape(1, depth))
    return pl.pallas_call(
        attention_kernel,
        grid=(heads, rows),
        out_shape=jax.ShapeDtypeStruct((rows, 2 * block, depth), jnp.bfloat16),
        in_specs=[
            whole(n),
            pl.BlockSpec((1,) + ball.shape[1:], lambda h, r: (h, 0, 0, 0, 0, 0, 0)),
        ] + [whole(a) for a in weights],
        out_specs=pl.BlockSpec((rows, 2 * block, depth), lambda h, r: (0, 0, 0)),
        scratch_shapes=[
            pltpu.VMEM((rows, keys, depth), jnp.bfloat16),
            pltpu.VMEM((rows, heads, size + 16, keys), jnp.bfloat16),
            pltpu.VMEM((rows, depth, 2 * block), jnp.bfloat16),
            pltpu.VMEM((rows, depth, 2 * block), jnp.float32),
            pltpu.VMEM((rows, depth, 2 * block), jnp.float32),
            pltpu.VMEM((keys, 2 * block), jnp.float32),
        ],
        compiler_params=pltpu.CompilerParams(vmem_limit_bytes=VMEM_LIMIT),
    )(n, ball, *weights)


def body(
    alignment_embedding,
    coupling_embedding,
    asking_projection,
    lookup_projection,
    content_projection,
    filter_projection,
    filter_offset,
    coupling_head_projection,
    final_projection,
    final_offset,
):
    rows, block, depth = alignment_embedding.shape
    tile = bias_tile(coupling_embedding, coupling_head_projection.T)
    normed = standardize_features(alignment_embedding).astype(jnp.bfloat16)
    nall, ball = exchange(normed, tile)
    update = attention(
        nall, ball, asking_projection, lookup_projection, content_projection, filter_projection,
        filter_offset, final_projection, final_offset,
    )
    zl = lax.axis_index("res") // 4
    qh = zl // 2
    mine = lax.dynamic_slice_in_dim(update, qh * block, block, axis=1)
    theirs = lax.dynamic_slice_in_dim(update, (1 - qh) * block, block, axis=1)
    swap = [(r, (r + 8) % 16) for r in range(16)]
    other = lax.ppermute(theirs, "res", swap)
    first = jnp.where(qh == 0, mine, other)
    second = jnp.where(qh == 0, other, mine)
    return jnp.concatenate([first, second], axis=0)


def solution(mesh):
    placed = (P("seq", "res", None), P("res", "seq", None), P(), P(), P(), P(), P(), P(), P(), P())
    return jax.shard_map(
        body, mesh=mesh, in_specs=placed, out_specs=P("seq", "res", None), check_vma=False
    )
```

```python
import jax
import jax.numpy as jnp
from jax import lax
from jax.experimental import pallas as pl
from jax.experimental.pallas import tpu as pltpu
from jax.sharding import PartitionSpec as P

MESH = pl.DeviceIdType.MESH
VMEM_LIMIT = 62 * 1024 * 1024
NT = (((1,), (1,)), ((), ()))
HEADS = 8
HALF = 4
BLOCK = 128
STEP = 256
TILES = (
    [(0, 0), (1, 0)]
    + [(0, 1), (1, 1)]
    + [(0, 2), (1, 2), (2, 0), (2, 1), (2, 2)]
    + [(0, 3), (1, 3), (2, 3)]
    + [(0, 4), (1, 4), (2, 4), (3, 0), (3, 1)]
    + [(0, 5), (1, 5), (2, 5), (3, 2)]
    + [(0, 6), (1, 6), (2, 6), (3, 3), (3, 4), (3, 5)]
    + [(3, 6), (0, 7), (1, 7), (2, 7), (3, 7)]
)
DONE = (
    (0, 0, 0), (0, 0, 0), (1, 1, 2), (3, 4, 4), (5, 6, 9), (10, 12, 12), (13, 15, 17), (18, 20, 21), (22, 27, 27),
    (32, 32, 32),
)


def lookup(table, index):
    value = jnp.int32(table[0])
    for at in range(1, len(table)):
        if table[at] != table[at - 1]:
            value = value + jnp.where(index >= at, table[at] - table[at - 1], 0).astype(jnp.int32)
    return value


def standardize_features(x):
    x = x.astype(jnp.float32)
    mean = jnp.mean(x, axis=-1, keepdims=True)
    var = jnp.mean((x - mean) ** 2, axis=-1, keepdims=True)
    return (x - mean) * lax.rsqrt(var + 1e-05)


def fused_kernel(
    m_ref, pair_ref, wq_ref, wk_ref, wv_ref, wf_ref, off_ref, wc_ref, wo_ref, oo_ref,
    out_ref,
    nown, nall, tile, ball, pair_buf, raw, k_scr, v_scr, q_scr, g_scr, a_scr, s_scr, upd, wqt, wvt,
    psem, lsem, zs, zr, xs, xr, bs, br, ys, yr, cs, cr, os, orr,
):
    s, res = lax.axis_index("seq"), lax.axis_index("res")
    c, y, zh, x, zl = s % 2, (s // 2) % 4, s // 8, res % 4, res // 4
    qh = zl // 2
    depth = wq_ref.shape[0]
    size = depth // HEADS
    keys = k_scr.shape[1]
    scale = 1.0 / size**0.5

    def device(c_=c, y_=y, zh_=zh, x_=x, zl_=zl):
        return (zh_ * 8 + y_ * 2 + c_, zl_ * 4 + x_)

    z_peers = [device(zl_=(zl + d) % 4) for d in (1, 2, 3)]
    x_left, x_right = device(x_=(x + 3) % 4), device(x_=(x + 1) % 4)
    y_left, y_right = device(y_=(y + 3) % 4), device(y_=(y + 1) % 4)
    partner = device(zl_=(zl + 2) % 4)
    b_peers = [partner, device(zh_=1 - zh), device(zh_=1 - zh, zl_=(zl + 2) % 4)]
    sibling = device(c_=1 - c)
    peers = z_peers + [x_left, x_right, y_left, y_right] + b_peers[1:] + [sibling]

    barrier = pltpu.get_barrier_semaphore()
    for peer in peers:
        pl.semaphore_signal(barrier, inc=1, device_id=peer, device_id_type=MESH)

    chunk = BLOCK // 4

    def pair_copy(i):
        at = pl.ds(i * chunk, chunk)
        return pltpu.make_async_copy(pair_ref.at[at], pair_buf.at[at], psem.at[i])

    for i in range(4):
        pair_copy(i).start()

    def norm_row(i, carry):
        nown[i] = standardize_features(m_ref[i]).astype(jnp.bfloat16)
        return carry

    lax.fori_loop(0, 2 * HALF, norm_row, 0)

    def remote(src, dst, send, recv, peer):
        return pltpu.make_async_remote_copy(
            src_ref=src, dst_ref=dst, send_sem=send, recv_sem=recv, device_id=peer, device_id_type=MESH
        )

    def z_copy(k, d):
        to = (zl + d + 1) % 4
        return remote(nown.at[(to // 2) * HALF + k], nall.at[k, x, zl], zs.at[k, d], zr.at[k, d], z_peers[d])

    def x_copy(k, d):
        return remote(nall.at[k, x], nall.at[k, x], xs.at[k, d], xr.at[k, d], (x_right, x_left)[d])

    def x_forward(k, d):
        block = nall.at[k, (x + 3) % 4, pl.ds(0, 2)] if d == 0 else nall.at[k, (x + 1) % 4, pl.ds(2, 2)]
        return remote(block, block, xs.at[k, 2 + d], xr.at[k, 2 + d], (x_right, x_left)[d])

    def b_copy(h, d):
        return remote(tile.at[h], ball.at[h, c, y, zh, qh], bs.at[h, d], br.at[h, d], b_peers[d])

    def y_copy(h, d):
        return remote(ball.at[h, c, y], ball.at[h, c, y], ys.at[h, d], yr.at[h, d], (y_right, y_left)[d])

    def y_forward(h, d):
        block = ball.at[h, c, (y + 3) % 4, 0] if d == 0 else ball.at[h, c, (y + 1) % 4, 1]
        return remote(block, block, ys.at[h, 2 + d], yr.at[h, 2 + d], (y_right, y_left)[d])

    def c_copy(h):
        return remote(ball.at[h, c], ball.at[h, c], cs.at[h], cr.at[h], sibling)

    def out_copy(r):
        return remote(
            upd.at[r, pl.ds((1 - qh) * BLOCK, BLOCK)], out_ref.at[qh * HALF + r], os.at[r], orr.at[r], partner
        )

    own_n = pltpu.make_async_copy(nown.at[pl.ds(qh * HALF, HALF)], nall.at[:, x, zl], lsem.at[0])
    own_b = pltpu.make_async_copy(tile, ball.at[:, c, y, zh, qh], lsem.at[1])

    pl.semaphore_wait(barrier, len(peers))
    own_n.start()

    def start_z(k, carry):
        for d in range(3):
            z_copy(k, d).start()
        return carry

    lax.fori_loop(0, HALF, start_z, 0)

    wqt[...] = wq_ref[...].astype(jnp.float32).T.astype(jnp.bfloat16)
    wvt[...] = wv_ref[...].astype(jnp.float32).T.astype(jnp.bfloat16)
    for r in range(HALF):
        v_scr[r, :, pl.ds(size, 16), :] = jnp.ones((HEADS, 16, keys), jnp.bfloat16)

    wc = wc_ref[...]
    group = 8

    def pair_rows(i, carry):
        at = pl.multiple_of(i * group, group)
        normed = standardize_features(pair_buf[pl.ds(at, group)]).astype(jnp.bfloat16)
        for j in range(group):
            raw[pl.ds(pl.multiple_of((at + j) * HEADS, HEADS), HEADS), :] = lax.dot_general(
                wc, normed[j], NT, preferred_element_type=jnp.float32
            )
        return carry

    def wait_z(k):
        for d in range(3):
            z_copy(k, d).wait_recv()
        for d in range(2):
            x_copy(k, d).start()

    for i in range(4):
        pair_copy(i).wait()
        lax.fori_loop(i * (chunk // group), (i + 1) * (chunk // group), pair_rows, 0)
        if i == 2:
            own_n.wait()
            wait_z(0)
    for h in range(HEADS):
        tile[h] = raw[pl.ds(h, BLOCK, stride=HEADS), :].T.astype(jnp.bfloat16)
    own_b.start()

    def start_b(h, carry):
        for d in range(3):
            b_copy(h, d).start()
        return carry

    lax.fori_loop(0, HEADS, start_b, 0)
    own_b.wait()

    def project(r):
        first = zl % 2
        rows_q = jnp.concatenate([nall[r, x, first], nall[r, x, first + 2]], axis=0)
        q = lax.dot_general(wqt[...], rows_q, NT, preferred_element_type=jnp.float32) * scale
        q_scr[r] = q.astype(jnp.bfloat16)
        g_scr[r] = jax.nn.sigmoid(
            jnp.dot(rows_q, wf_ref[...], preferred_element_type=jnp.float32) + off_ref[...]
        )

        def part(i, carry):
            rows = nall[r, i].reshape(4 * BLOCK, depth)
            at = pl.multiple_of(i * 4 * BLOCK, 4 * BLOCK)
            k_scr[r, pl.ds(at, 4 * BLOCK), :] = jnp.dot(
                rows, wk_ref[...], preferred_element_type=jnp.float32
            ).astype(jnp.bfloat16)
            v = lax.dot_general(wvt[...], rows, NT, preferred_element_type=jnp.float32).astype(jnp.bfloat16)
            for h in range(HEADS):
                v_scr[r, h, pl.ds(0, size), pl.ds(at, 4 * BLOCK)] = v[h * size:(h + 1) * size]
            return carry

        lax.fori_loop(0, 4, part, 0)

    def attend(r, h):
        qt = q_scr[r]
        channel = lax.broadcasted_iota(jnp.int32, qt.shape, 0)
        qm = jnp.where((channel >= h * size) & (channel < (h + 1) * size), qt, jnp.zeros_like(qt))
        top = None
        for at in range(0, keys, STEP):
            scores = jnp.dot(k_scr[r, pl.ds(at, STEP), :], qm, preferred_element_type=jnp.float32)
            parts = []
            for sub in range(at // BLOCK, (at + STEP) // BLOCK):
                j = (sub % 4) * 4 + sub // 4
                here = (h, j % 2, (j // 2) % 4, j // 8)
                parts.append(jnp.concatenate([ball[here + (0,)], ball[here + (1,)]], axis=1))
            scores = scores + jnp.concatenate(parts, axis=0).astype(jnp.float32)
            s_scr[pl.ds(at, STEP), :] = scores
            best = jnp.max(scores, axis=0, keepdims=True)
            top = best if top is None else jnp.maximum(top, best)
        acc = None
        for at in range(0, keys, STEP):
            weights = jnp.exp(s_scr[pl.ds(at, STEP), :] - top).astype(jnp.bfloat16)
            part = jnp.dot(v_scr[r, h, :, pl.ds(at, STEP)], weights, preferred_element_type=jnp.float32)
            acc = part if acc is None else acc + part
        a_scr[r, pl.ds(pl.multiple_of(h * size, size), size), :] = acc[:size] / acc[size:size + 1]

    def finish(r):
        gated = (g_scr[r] * a_scr[r].T).astype(jnp.bfloat16)
        update = jnp.dot(gated, wo_ref[...], preferred_element_type=jnp.float32) + oo_ref[...]
        upd[r] = update.astype(jnp.bfloat16)
        out_copy(r).start()
        out_ref[qh * HALF + r] = upd[r, pl.ds(pl.multiple_of(qh * BLOCK, BLOCK), BLOCK), :]

    tile_rows, tile_heads = [t[0] for t in TILES], [t[1] for t in TILES]

    def run_tile(i, carry):
        r, h = lookup(tile_rows, i), lookup(tile_heads, i)
        attend(r, h)
        pl.when(h == HEADS - 1)(lambda: finish(r))
        return carry

    def run_tiles(first, last):
        lax.fori_loop(first, last, run_tile, 0)

    def tick(t, done):
        even = t % 2 == 0
        k = t // 2
        after = [lookup([d[p] for d in DONE], t) for p in range(3)]

        @pl.when(t < HEADS)
        def _():
            for d in range(3):
                b_copy(t, d).wait_recv()
            for d in range(2):
                y_copy(t, d).start()

        @pl.when(even & (k < HALF))
        def _():
            for d in range(2):
                x_copy(k, d).wait_recv()
            for d in range(2):
                x_forward(k, d).start()

        @pl.when(t >= 2)
        def _():
            c_copy(t - 2).wait_recv()

        run_tiles(done, after[0])

        @pl.when((t >= 1) & (t <= HEADS))
        def _():
            for d in range(2):
                y_forward(t - 1, d).wait_recv()
            c_copy(t - 1).start()

        @pl.when(even & (k < HALF - 1))
        def _():
            wait_z(k + 1)

        run_tiles(after[0], after[1])

        @pl.when(t < HEADS)
        def _():
            for d in range(2):
                y_copy(t, d).wait_recv()
            for d in range(2):
                y_forward(t, d).start()

        @pl.when(even & (k < HALF))
        def _():
            for d in range(2):
                x_forward(k, d).wait_recv()
            project(k)

        run_tiles(after[1], after[2])
        return after[2]

    lax.fori_loop(0, len(DONE), tick, jnp.int32(0))

    def close_rows(k, carry):
        out_copy(k).wait_recv()
        out_copy(k).wait_send()
        for d in range(3):
            z_copy(k, d).wait_send()
        for d in range(2):
            x_copy(k, d).wait_send()
            x_forward(k, d).wait_send()
        return carry

    def close_heads(h, carry):
        for d in range(3):
            b_copy(h, d).wait_send()
        for d in range(2):
            y_copy(h, d).wait_send()
            y_forward(h, d).wait_send()
        c_copy(h).wait_send()
        return carry

    lax.fori_loop(0, HEADS, close_heads, 0)
    lax.fori_loop(0, HALF, close_rows, 0)


def body(
    alignment_embedding,
    coupling_embedding,
    asking_projection,
    lookup_projection,
    content_projection,
    filter_projection,
    filter_offset,
    coupling_head_projection,
    final_projection,
    final_offset,
):
    rows, block, depth = alignment_embedding.shape
    heads = coupling_head_projection.shape[1]
    size = depth // heads
    keys = 16 * block
    bf, f32 = jnp.bfloat16, jnp.float32
    sem = pltpu.SemaphoreType.DMA
    vmem = pl.BlockSpec(memory_space=pltpu.VMEM)
    in_specs = [vmem] * 10
    in_specs[1] = pl.BlockSpec(memory_space=pl.ANY)
    return pl.pallas_call(
        fused_kernel,
        out_shape=jax.ShapeDtypeStruct((rows, block, depth), bf),
        in_specs=in_specs,
        out_specs=vmem,
        scratch_shapes=[
            pltpu.VMEM((rows, block, depth), bf),
            pltpu.VMEM((HALF, 4, 4, block, depth), bf),
            pltpu.VMEM((heads, block, block), bf),
            pltpu.VMEM((heads, 2, 4, 2, 2, block, block), bf),
            pltpu.VMEM((block, block, coupling_embedding.shape[2]), bf),
            pltpu.VMEM((block * heads, block), f32),
            pltpu.VMEM((HALF, keys, depth), bf),
            pltpu.VMEM((HALF, heads, size + 16, keys), bf),
            pltpu.VMEM((HALF, depth, 2 * block), bf),
            pltpu.VMEM((HALF, 2 * block, depth), f32),
            pltpu.VMEM((HALF, depth, 2 * block), f32),
            pltpu.VMEM((keys, 2 * block), f32),
            pltpu.VMEM((HALF, 2 * block, depth), bf),
            pltpu.VMEM((depth, depth), bf),
            pltpu.VMEM((depth, depth), bf),
            sem((4,)),
            sem((2,)),
            sem((HALF, 3)),
            sem((HALF, 3)),
            sem((HALF, 4)),
            sem((HALF, 4)),
            sem((heads, 3)),
            sem((heads, 3)),
            sem((heads, 4)),
            sem((heads, 4)),
            sem((heads,)),
            sem((heads,)),
            sem((HALF,)),
            sem((HALF,)),
        ],
        compiler_params=pltpu.CompilerParams(
            collective_id=0, has_side_effects=True, vmem_limit_bytes=VMEM_LIMIT
        ),
    )(
        alignment_embedding, coupling_embedding, asking_projection, lookup_projection, content_projection,
        filter_projection, filter_offset.reshape(1, depth), coupling_head_projection.T, final_projection,
        final_offset.reshape(1, depth),
    )


def solution(mesh):
    placed = (P("seq", "res", None), P("res", "seq", None), P(), P(), P(), P(), P(), P(), P(), P())
    return jax.shard_map(
        body, mesh=mesh, in_specs=placed, out_specs=P("seq", "res", None), check_vma=False
    )
```

```python
import jax
import jax.numpy as jnp
from jax import lax
from jax.experimental import pallas as pl
from jax.experimental.pallas import tpu as pltpu
from jax.sharding import PartitionSpec as P

MESH = pl.DeviceIdType.MESH
VMEM_LIMIT = 62 * 1024 * 1024
NT = (((1,), (1,)), ((), ()))
HEADS = 8
HALF = 4
BLOCK = 128
STEP = 256
STEPS = (
    0, 1, 3, 3, 4, 1, 3, 4, 2, 5, 2, 0, 6, 4, 7, 7, 5, 3, 5, 6, 7, 3, 7, 6, 7,
    4, 7, 1, 0, 4, 5, 3, 2, 6, 5, 7, 3, 7, 7, 6, 4, 7, 3, 1, 7, 7, 4, 7, 7, 5,
    7, 2, 4, 6, 7, 5, 7, 7, 7, 6, 5, 7, 7, 7, 6, 7, 7, 7, 7, 7, 7, 7, 7, 7, 7,
)
TILES = (
    0, 8, 1, 9, 2, 10, 16, 17, 18, 3, 11, 19, 4, 12, 20, 24,
    25, 26, 27, 28, 5, 13, 21, 29, 6, 14, 22, 30, 7, 15, 23, 31,
)


def packed(values, bits):
    per = 30 // bits
    return per, [sum(v << (bits * at) for at, v in enumerate(values[i:i + per])) for i in range(0, len(values), per)]


def unpacked(values, bits, index):
    per, words = packed(values, bits)
    word = lookup(words, index // per)
    return (word >> (bits * (index % per))) % (1 << bits)


def lookup(table, index):
    value = jnp.int32(table[0])
    for at in range(1, len(table)):
        value = jnp.where(index >= at, jnp.int32(table[at]), value)
    return value


def standardize_features(x):
    x = x.astype(jnp.float32)
    mean = jnp.mean(x, axis=-1, keepdims=True)
    var = jnp.mean((x - mean) ** 2, axis=-1, keepdims=True)
    return (x - mean) * lax.rsqrt(var + 1e-05)


def fused_kernel(
    m_ref, pair_ref, wq_ref, wk_ref, wv_ref, wf_ref, off_ref, wc_ref, wo_ref, oo_ref,
    out_ref,
    nown, nall, tile, ball, pair_buf, raw, k_scr, v_scr, q_scr, g_scr, a_scr, s_even, s_odd, t_even, t_odd, upd, wqt, wvt,
    psem, lsem, zs, zr, xs, xr, bs, br, ys, yr, cs, cr, os, orr,
):
    s, res = lax.axis_index("seq"), lax.axis_index("res")
    c, y, zh, x, zl = s % 2, (s // 2) % 4, s // 8, res % 4, res // 4
    qh = zl // 2
    depth = wq_ref.shape[0]
    size = depth // HEADS
    keys = k_scr.shape[1]
    scale = 1.0 / size**0.5

    def device(c_=c, y_=y, zh_=zh, x_=x, zl_=zl):
        return (zh_ * 8 + y_ * 2 + c_, zl_ * 4 + x_)

    z_peers = [device(zl_=(zl + d) % 4) for d in (1, 2, 3)]
    x_left, x_right = device(x_=(x + 3) % 4), device(x_=(x + 1) % 4)
    y_left, y_right = device(y_=(y + 3) % 4), device(y_=(y + 1) % 4)
    partner = device(zl_=(zl + 2) % 4)
    b_peers = [partner, device(zh_=1 - zh), device(zh_=1 - zh, zl_=(zl + 2) % 4)]
    sibling = device(c_=1 - c)
    peers = z_peers + [x_left, x_right, y_left, y_right] + b_peers[1:] + [sibling]

    barrier = pltpu.get_barrier_semaphore()
    for peer in peers:
        pl.semaphore_signal(barrier, inc=1, device_id=peer, device_id_type=MESH)

    chunk = BLOCK // 4

    def pair_copy(i):
        at = pl.ds(i * chunk, chunk)
        return pltpu.make_async_copy(pair_ref.at[at], pair_buf.at[at], psem.at[i])

    for i in range(4):
        pair_copy(i).start()

    def norm_row(i, carry):
        nown[i] = standardize_features(m_ref[i]).astype(jnp.bfloat16)
        return carry

    lax.fori_loop(0, 2 * HALF, norm_row, 0)

    def remote(src, dst, send, recv, peer):
        return pltpu.make_async_remote_copy(
            src_ref=src, dst_ref=dst, send_sem=send, recv_sem=recv, device_id=peer, device_id_type=MESH
        )

    def z_copy(k, d):
        to = (zl + d + 1) % 4
        return remote(nown.at[(to // 2) * HALF + k], nall.at[k, x, zl], zs.at[k, d], zr.at[k, d], z_peers[d])

    def x_copy(k, d):
        return remote(nall.at[k, x], nall.at[k, x], xs.at[k, d], xr.at[k, d], (x_right, x_left)[d])

    def x_forward(k, d):
        block = nall.at[k, (x + 3) % 4, pl.ds(0, 2)] if d == 0 else nall.at[k, (x + 1) % 4, pl.ds(2, 2)]
        return remote(block, block, xs.at[k, 2 + d], xr.at[k, 2 + d], (x_right, x_left)[d])

    def b_copy(h, d):
        return remote(tile.at[h], ball.at[h, c, y, zh, qh], bs.at[h, d], br.at[h, d], b_peers[d])

    def y_copy(h, d):
        return remote(ball.at[h, c, y], ball.at[h, c, y], ys.at[h, d], yr.at[h, d], (y_right, y_left)[d])

    def y_forward(h, d):
        block = ball.at[h, c, (y + 3) % 4, 0] if d == 0 else ball.at[h, c, (y + 1) % 4, 1]
        return remote(block, block, ys.at[h, 2 + d], yr.at[h, 2 + d], (y_right, y_left)[d])

    def c_copy(h):
        return remote(ball.at[h, c], ball.at[h, c], cs.at[h], cr.at[h], sibling)

    def out_copy(r):
        return remote(
            upd.at[r, pl.ds((1 - qh) * BLOCK, BLOCK)], out_ref.at[qh * HALF + r], os.at[r], orr.at[r], partner
        )

    own_n = pltpu.make_async_copy(nown.at[pl.ds(qh * HALF, HALF)], nall.at[:, x, zl], lsem.at[0])
    own_b = pltpu.make_async_copy(tile, ball.at[:, c, y, zh, qh], lsem.at[1])

    pl.semaphore_wait(barrier, len(peers))
    own_n.start()

    def start_z(k):
        for d in range(3):
            z_copy(k, d).start()

    start_z(0)
    start_z(1)

    wqt[...] = wq_ref[...].astype(jnp.float32).T.astype(jnp.bfloat16)
    wvt[...] = wv_ref[...].astype(jnp.float32).T.astype(jnp.bfloat16)
    for r in range(HALF):
        v_scr[r, :, pl.ds(size, 16), :] = jnp.ones((HEADS, 16, keys), jnp.bfloat16)

    wc = wc_ref[...]
    group = 8

    def pair_rows(i, carry):
        at = pl.multiple_of(i * group, group)
        normed = standardize_features(pair_buf[pl.ds(at, group)]).astype(jnp.bfloat16)
        for j in range(group):
            raw[pl.ds(pl.multiple_of((at + j) * HEADS, HEADS), HEADS), :] = lax.dot_general(
                wc, normed[j], NT, preferred_element_type=jnp.float32
            )
        return carry

    def wait_z(k):
        for d in range(3):
            z_copy(k, d).wait_recv()
        for d in range(2):
            x_copy(k, d).start()

    for i in range(4):
        pair_copy(i).wait()
        lax.fori_loop(i * (chunk // group), (i + 1) * (chunk // group), pair_rows, 0)
        if i == 2:
            own_n.wait()
            wait_z(0)
    for h in range(HEADS):
        tile[h] = raw[pl.ds(h, BLOCK, stride=HEADS), :].T.astype(jnp.bfloat16)
    own_b.start()

    def start_b(h):
        for d in range(3):
            b_copy(h, d).start()

    start_b(0)
    start_b(1)
    start_b(2)
    start_z(2)
    start_b(3)
    start_b(4)
    start_z(3)
    start_b(5)
    start_b(6)
    start_b(7)
    own_b.wait()

    def project(r):
        first = zl % 2
        rows_q = jnp.concatenate([nall[r, x, first], nall[r, x, first + 2]], axis=0)
        q = lax.dot_general(wqt[...], rows_q, NT, preferred_element_type=jnp.float32) * scale
        q_scr[r] = q.astype(jnp.bfloat16)
        g_scr[r] = jax.nn.sigmoid(
            jnp.dot(rows_q, wf_ref[...], preferred_element_type=jnp.float32) + off_ref[...]
        )

        def part(i, carry):
            rows = nall[r, i].reshape(4 * BLOCK, depth)
            at = pl.multiple_of(i * 4 * BLOCK, 4 * BLOCK)
            k_scr[r, pl.ds(at, 4 * BLOCK), :] = jnp.dot(
                rows, wk_ref[...], preferred_element_type=jnp.float32
            ).astype(jnp.bfloat16)
            v = lax.dot_general(wvt[...], rows, NT, preferred_element_type=jnp.float32).astype(jnp.bfloat16)
            for h in range(HEADS):
                v_scr[r, h, pl.ds(0, size), pl.ds(at, 4 * BLOCK)] = v[h * size:(h + 1) * size]
            return carry

        lax.fori_loop(0, 4, part, 0)

    def scores(r, h):
        qt = q_scr[r]
        channel = lax.broadcasted_iota(jnp.int32, qt.shape, 0)
        qm = jnp.where((channel >= h * size) & (channel < (h + 1) * size), qt, jnp.zeros_like(qt))

        def block(at, s_ref, top):
            part = jnp.dot(k_scr[r, pl.ds(at, STEP), :], qm, preferred_element_type=jnp.float32)
            biases = []
            for sub in range(at // BLOCK, (at + STEP) // BLOCK):
                j = (sub % 4) * 4 + sub // 4
                here = (h, j % 2, (j // 2) % 4, j // 8)
                biases.append(jnp.concatenate([ball[here + (0,)], ball[here + (1,)]], axis=1))
            part = part + jnp.concatenate(biases, axis=0).astype(jnp.float32)
            s_ref[pl.ds(at, STEP), :] = part
            best = jnp.max(part.reshape(STEP // 8, 8, part.shape[1]), axis=0)
            return best if top is None else jnp.maximum(top, best)

        return block

    def mix(r, h, t_ref):
        top = jnp.max(t_ref[...], axis=0, keepdims=True)

        def block(at, s_ref, acc):
            weights = jnp.exp(s_ref[pl.ds(at, STEP), :] - top).astype(jnp.bfloat16)
            part = jnp.dot(v_scr[r, h, :, pl.ds(at, STEP)], weights, preferred_element_type=jnp.float32)
            return part if acc is None else acc + part

        return block

    def attend(new, s_new, t_new, old, s_old, t_old):
        top = acc = None
        score = None if new is None else scores(*new)
        mixed = None if old is None else mix(*old, t_old)
        for at in range(0, keys, STEP):
            if score is not None:
                top = score(at, s_new, top)
            if mixed is not None:
                acc = mixed(at, s_old, acc)
        if score is not None:
            t_new[...] = top
        if mixed is not None:
            r, h = old
            a_scr[r, pl.ds(pl.multiple_of(h * size, size), size), :] = acc[:size] / acc[size:size + 1]

    def finish(r):
        gated = (g_scr[r] * a_scr[r].T).astype(jnp.bfloat16)
        update = jnp.dot(gated, wo_ref[...], preferred_element_type=jnp.float32) + oo_ref[...]
        upd[r] = update.astype(jnp.bfloat16)
        out_copy(r).start()
        out_ref[qh * HALF + r] = upd[r, pl.ds(pl.multiple_of(qh * BLOCK, BLOCK), BLOCK), :]

    def row_z(k):
        wait_z(k)

    def row_x(k):
        for d in range(2):
            x_copy(k, d).wait_recv()
        for d in range(2):
            x_forward(k, d).start()

    def row_last(k):
        for d in range(2):
            x_forward(k, d).wait_recv()
        project(k)

    def head_z(h):
        for d in range(3):
            b_copy(h, d).wait_recv()
        for d in range(2):
            y_copy(h, d).start()

    def head_y(h):
        for d in range(2):
            y_copy(h, d).wait_recv()
        for d in range(2):
            y_forward(h, d).start()

    def head_last(h):
        for d in range(2):
            y_forward(h, d).wait_recv()
        c_copy(h).start()

    def head_core(h):
        c_copy(h).wait_recv()

    def tile_at(i):
        at = unpacked(TILES, 5, i)
        return at // HEADS, at % HEADS

    even, odd = (s_even, t_even), (s_odd, t_odd)

    def run_tile(i):
        new, old = tile_at(i), tile_at(jnp.maximum(i - 1, 0))
        pl.when(i == 0)(lambda: attend(new, *even, None, *odd))
        pl.when(i % 2 == 1)(lambda: attend(new, *odd, old, *even))
        pl.when((i > 0) & (i % 2 == 0))(lambda: attend(new, *even, old, *odd))
        pl.when((i > 0) & (old[1] == HEADS - 1))(lambda: finish(old[0]))

    actions = (row_z, row_x, row_last, head_z, head_y, head_last, head_core, run_tile)

    def step(n, counts):
        kind = unpacked(STEPS, 3, n)
        for at, action in enumerate(actions):
            pl.when(kind == at)(lambda action=action, at=at: action(counts[at]))
        return tuple(count + (kind == at).astype(jnp.int32) for at, count in enumerate(counts))

    lax.fori_loop(0, len(STEPS), step, (jnp.int32(1),) + (jnp.int32(0),) * 7)
    last = (TILES[-1] // HEADS, TILES[-1] % HEADS)
    attend(None, *even, last, *odd)
    finish(last[0])

    def close_rows(k, carry):
        out_copy(k).wait_recv()
        out_copy(k).wait_send()
        for d in range(3):
            z_copy(k, d).wait_send()
        for d in range(2):
            x_copy(k, d).wait_send()
            x_forward(k, d).wait_send()
        return carry

    def close_heads(h, carry):
        for d in range(3):
            b_copy(h, d).wait_send()
        for d in range(2):
            y_copy(h, d).wait_send()
            y_forward(h, d).wait_send()
        c_copy(h).wait_send()
        return carry

    lax.fori_loop(0, HEADS, close_heads, 0)
    lax.fori_loop(0, HALF, close_rows, 0)


def body(
    alignment_embedding,
    coupling_embedding,
    asking_projection,
    lookup_projection,
    content_projection,
    filter_projection,
    filter_offset,
    coupling_head_projection,
    final_projection,
    final_offset,
):
    rows, block, depth = alignment_embedding.shape
    heads = coupling_head_projection.shape[1]
    size = depth // heads
    keys = 16 * block
    bf, f32 = jnp.bfloat16, jnp.float32
    sem = pltpu.SemaphoreType.DMA
    vmem = pl.BlockSpec(memory_space=pltpu.VMEM)
    in_specs = [vmem] * 10
    in_specs[1] = pl.BlockSpec(memory_space=pl.ANY)
    return pl.pallas_call(
        fused_kernel,
        out_shape=jax.ShapeDtypeStruct((rows, block, depth), bf),
        in_specs=in_specs,
        out_specs=vmem,
        scratch_shapes=[
            pltpu.VMEM((rows, block, depth), bf),
            pltpu.VMEM((HALF, 4, 4, block, depth), bf),
            pltpu.VMEM((heads, block, block), bf),
            pltpu.VMEM((heads, 2, 4, 2, 2, block, block), bf),
            pltpu.VMEM((block, block, coupling_embedding.shape[2]), bf),
            pltpu.VMEM((block * heads, block), f32),
            pltpu.VMEM((HALF, keys, depth), bf),
            pltpu.VMEM((HALF, heads, size + 16, keys), bf),
            pltpu.VMEM((HALF, depth, 2 * block), bf),
            pltpu.VMEM((HALF, 2 * block, depth), f32),
            pltpu.VMEM((HALF, depth, 2 * block), f32),
            pltpu.VMEM((keys, 2 * block), f32),
            pltpu.VMEM((keys, 2 * block), f32),
            pltpu.VMEM((8, 2 * block), f32),
            pltpu.VMEM((8, 2 * block), f32),
            pltpu.VMEM((HALF, 2 * block, depth), bf),
            pltpu.VMEM((depth, depth), bf),
            pltpu.VMEM((depth, depth), bf),
            sem((4,)),
            sem((2,)),
            sem((HALF, 3)),
            sem((HALF, 3)),
            sem((HALF, 4)),
            sem((HALF, 4)),
            sem((heads, 3)),
            sem((heads, 3)),
            sem((heads, 4)),
            sem((heads, 4)),
            sem((heads,)),
            sem((heads,)),
            sem((HALF,)),
            sem((HALF,)),
        ],
        compiler_params=pltpu.CompilerParams(
            collective_id=0, has_side_effects=True, vmem_limit_bytes=VMEM_LIMIT
        ),
    )(
        alignment_embedding, coupling_embedding, asking_projection, lookup_projection, content_projection,
        filter_projection, filter_offset.reshape(1, depth), coupling_head_projection.T, final_projection,
        final_offset.reshape(1, depth),
    )


def solution(mesh):
    placed = (P("seq", "res", None), P("res", "seq", None), P(), P(), P(), P(), P(), P(), P(), P())
    return jax.shard_map(
        body, mesh=mesh, in_specs=placed, out_specs=P("seq", "res", None), check_vma=False
    )
```

```python
import jax
import jax.numpy as jnp
from jax import lax
from jax.experimental import pallas as pl
from jax.experimental.pallas import tpu as pltpu
from jax.sharding import PartitionSpec as P

MESH = pl.DeviceIdType.MESH
VMEM_LIMIT = 62 * 1024 * 1024
NT = (((1,), (1,)), ((), ()))
HEADS = 8
HALF = 4
BLOCK = 128
STEP = 256
FORWARDED = (2, 6)
STEPS = (
    0, 6, 2, 2, 1, 6, 3, 4, 6, 0, 6, 6, 5, 7, 2, 3, 4, 2, 5, 7, 3, 0, 6, 3, 1,
    6, 6, 4, 6, 7, 2, 7, 5, 7, 4, 7, 2, 5, 7, 7, 3, 0, 6, 3, 1, 6, 6, 6, 7, 4,
    2, 7, 7, 7, 4, 5, 2, 7, 7, 7, 5, 7, 7, 7, 3, 4, 1, 6, 6, 6, 7, 5, 7, 7, 3,
    4, 7, 7, 7, 5, 7, 7, 7, 7, 7, 7, 7, 7,
)
TILES = (
    0, 1, 8, 9, 2, 10, 3, 11, 16, 17, 18, 19, 4, 12, 20, 5,
    13, 21, 24, 25, 26, 27, 28, 29, 6, 14, 22, 30, 7, 15, 23, 31,
)
PARTS = (
    0, 1, 2, 3, 4, 8, 5, 6, 7, 12, 9, 10, 11, 13, 14, 15,
)


def forwarded(h):
    return (h >= FORWARDED[0]) & (h < FORWARDED[1])


def packed(values, bits):
    per = 30 // bits
    return per, [sum(v << (bits * at) for at, v in enumerate(values[i:i + per])) for i in range(0, len(values), per)]


def unpacked(values, bits, index):
    per, words = packed(values, bits)
    word = lookup(words, index // per)
    return (word >> (bits * (index % per))) % (1 << bits)


def lookup(table, index):
    value = jnp.int32(table[0])
    for at in range(1, len(table)):
        value = jnp.where(index >= at, jnp.int32(table[at]), value)
    return value


def standardize_features(x):
    x = x.astype(jnp.float32)
    mean = jnp.mean(x, axis=-1, keepdims=True)
    var = jnp.mean((x - mean) ** 2, axis=-1, keepdims=True)
    return (x - mean) * lax.rsqrt(var + 1e-05)


def fused_kernel(
    m_ref, pair_ref, wq_ref, wk_ref, wv_ref, wf_ref, off_ref, wc_ref, wo_ref, oo_ref,
    out_ref,
    nown, nall, tile, ball, pair_buf, raw, k_scr, v_scr, q_scr, g_scr, g_own, g_send, s_even, s_odd, t_even, t_odd, wqt, wvt, wft, wot, offsets,
    psem, lsem, zs, zr, xs, xr, bs, br, ys, yr, cs, cr, os, orr,
):
    s, res = lax.axis_index("seq"), lax.axis_index("res")
    c, y, zh, x, zl = s % 2, (s // 2) % 4, s // 8, res % 4, res // 4
    qh = zl // 2
    depth = wq_ref.shape[0]
    size = depth // HEADS
    keys = k_scr.shape[1]
    scale = 1.0 / size**0.5

    def device(c_=c, y_=y, zh_=zh, x_=x, zl_=zl):
        return (zh_ * 8 + y_ * 2 + c_, zl_ * 4 + x_)

    z_peers = [device(zl_=(zl + d) % 4) for d in (1, 2, 3)]
    x_peers = [device(x_=(x + d) % 4) for d in (1, 2, 3)]
    y_peers = [device(y_=(y + d) % 4) for d in (1, 2, 3)]
    partner = device(zl_=(zl + 2) % 4)
    b_peers = [partner, device(zh_=1 - zh), device(zh_=1 - zh, zl_=(zl + 2) % 4)]
    sibling = device(c_=1 - c)
    peers = z_peers + x_peers + y_peers + b_peers[1:] + [sibling]

    barrier = pltpu.get_barrier_semaphore()
    for peer in peers:
        pl.semaphore_signal(barrier, inc=1, device_id=peer, device_id_type=MESH)

    chunk = BLOCK // 4

    def pair_copy(i):
        at = pl.ds(i * chunk, chunk)
        return pltpu.make_async_copy(pair_ref.at[at], pair_buf.at[at], psem.at[i])

    for i in range(4):
        pair_copy(i).start()

    def norm_rows(k, carry):
        for i in (k, HALF + k):
            nown[i] = standardize_features(m_ref[i]).astype(jnp.bfloat16)
        return carry

    norm_rows(0, 0)

    def remote(src, dst, send, recv, peer):
        return pltpu.make_async_remote_copy(
            src_ref=src, dst_ref=dst, send_sem=send, recv_sem=recv, device_id=peer, device_id_type=MESH
        )

    def z_copy(k, d):
        to = (zl + d + 1) % 4
        return remote(nown.at[(to // 2) * HALF + k], nall.at[k, x, zl], zs.at[k, d], zr.at[k, d], z_peers[d])

    def x_copy(k, d):
        return remote(nall.at[k, x], nall.at[k, x], xs.at[k, d], xr.at[k, d], x_peers[d])

    def b_copy(h, d):
        return remote(tile.at[h], ball.at[h, c, y, zh, qh], bs.at[h, d], br.at[h, d], b_peers[d])

    def y_copy(h, d):
        return remote(ball.at[h, c, y], ball.at[h, c, y], ys.at[h, d], yr.at[h, d], y_peers[d])

    def y_forward(h, d):
        block = ball.at[h, c, (y + 3) % 4, 0] if d == 0 else ball.at[h, c, (y + 1) % 4, 1]
        return remote(block, block, ys.at[h, 1 + 2 * d], yr.at[h, 1 + 2 * d], y_peers[2 * d])

    def c_copy(h):
        return remote(ball.at[h, c], ball.at[h, c], cs.at[h], cr.at[h], sibling)

    def g_copy(r, h):
        at = pl.ds(pl.multiple_of(h * size, size), size)
        return remote(g_send.at[r, at], g_own.at[qh * HALF + r, at], os.at[r, h], orr.at[r, h], partner)

    own_n = pltpu.make_async_copy(nown.at[pl.ds(qh * HALF, HALF)], nall.at[:, x, zl], lsem.at[0])
    own_b = pltpu.make_async_copy(tile, ball.at[:, c, y, zh, qh], lsem.at[1])

    pl.semaphore_wait(barrier, len(peers))

    def start_z(k):
        for d in range(3):
            z_copy(k, d).start()

    start_z(0)

    wc = wc_ref[...]
    group = 16

    def pair_rows(i, carry):
        at = pl.multiple_of(i * group, group)
        normed = standardize_features(pair_buf[pl.ds(at, group)]).astype(jnp.bfloat16)
        for j in range(group):
            raw[pl.ds(pl.multiple_of((at + j) * HEADS, HEADS), HEADS), :] = lax.dot_general(
                wc, normed[j], NT, preferred_element_type=jnp.float32
            )
        return carry

    def gates(r):
        first = zl % 2
        rows_q = jnp.concatenate([nall[r, x, first], nall[r, x, first + 2]], axis=0)
        q = lax.dot_general(wqt[...], rows_q, NT, preferred_element_type=jnp.float32) * scale
        q_scr[r] = q.astype(jnp.bfloat16)
        gate = lax.dot_general(wft[...], rows_q, NT, preferred_element_type=jnp.float32)
        offset = jnp.concatenate([offsets[...], offsets[...]], axis=1)
        g_scr[r] = jax.nn.sigmoid(gate + offset)

    def project(r, i):
        rows = nall[r, i].reshape(4 * BLOCK, depth)
        at = pl.multiple_of(i * 4 * BLOCK, 4 * BLOCK)
        k_scr[r, pl.ds(at, 4 * BLOCK), :] = jnp.dot(
            rows, wk_ref[...], preferred_element_type=jnp.float32
        ).astype(jnp.bfloat16)
        v = lax.dot_general(wvt[...], rows, NT, preferred_element_type=jnp.float32).astype(jnp.bfloat16)
        for h in range(HEADS):
            v_scr[r, h, pl.ds(0, size), pl.ds(at, 4 * BLOCK)] = v[h * size:(h + 1) * size]

    def row_z(k):
        for d in range(3):
            z_copy(k, d).wait_recv()
        for d in range(3):
            x_copy(k, d).start()

    for i in range(4):
        pair_copy(i).wait()
        lax.fori_loop(i * (chunk // group), (i + 1) * (chunk // group), pair_rows, 0)
    for h in range(HEADS):
        tile[h] = raw[pl.ds(h, BLOCK, stride=HEADS), :].T.astype(jnp.bfloat16)
    own_b.start()

    def start_b(h):
        for d in range(3):
            b_copy(h, d).start()

    start_b(0)
    start_b(1)
    lax.fori_loop(1, HALF, norm_rows, 0)
    own_n.start()
    start_z(1)
    start_b(2)
    start_b(3)
    start_z(2)
    start_b(4)
    start_b(5)
    start_z(3)
    start_b(6)
    start_b(7)
    wqt[...] = wq_ref[...].astype(jnp.float32).T.astype(jnp.bfloat16)
    wvt[...] = wv_ref[...].astype(jnp.float32).T.astype(jnp.bfloat16)
    wft[...] = wf_ref[...].astype(jnp.float32).T.astype(jnp.bfloat16)
    wot[...] = wo_ref[...].astype(jnp.float32).T.astype(jnp.bfloat16)
    offsets[...] = jnp.broadcast_to(off_ref[...], (BLOCK, depth)).T
    for r in range(HALF):
        v_scr[r, :, pl.ds(size, 16), :] = jnp.ones((HEADS, 16, keys), jnp.bfloat16)

    own_n.wait()
    own_b.wait()

    def scores(r, h):
        qt = q_scr[r]
        channel = lax.broadcasted_iota(jnp.int32, qt.shape, 0)
        qm = jnp.where((channel >= h * size) & (channel < (h + 1) * size), qt, jnp.zeros_like(qt))

        def block(at, s_ref, top):
            part = jnp.dot(k_scr[r, pl.ds(at, STEP), :], qm, preferred_element_type=jnp.float32)
            biases = []
            for sub in range(at // BLOCK, (at + STEP) // BLOCK):
                j = (sub % 4) * 4 + sub // 4
                here = (h, j % 2, (j // 2) % 4, j // 8)
                biases.append(jnp.concatenate([ball[here + (0,)], ball[here + (1,)]], axis=1))
            part = part + jnp.concatenate(biases, axis=0).astype(jnp.float32)
            s_ref[pl.ds(at, STEP), :] = part
            best = jnp.max(part.reshape(STEP // 8, 8, part.shape[1]), axis=0)
            return best if top is None else jnp.maximum(top, best)

        return block

    def mix(r, h, t_ref):
        top = jnp.max(t_ref[...], axis=0, keepdims=True)

        def block(at, s_ref, acc):
            weights = jnp.exp(s_ref[pl.ds(at, STEP), :] - top).astype(jnp.bfloat16)
            part = jnp.dot(v_scr[r, h, :, pl.ds(at, STEP)], weights, preferred_element_type=jnp.float32)
            return part if acc is None else acc + part

        return block

    def attend(new, s_new, t_new, old, s_old, t_old):
        top = acc = None
        score = None if new is None else scores(*new)
        mixed = None if old is None else mix(*old, t_old)
        for at in range(0, keys, STEP):
            if score is not None:
                top = score(at, s_new, top)
            if mixed is not None:
                acc = mixed(at, s_old, acc)
        if score is not None:
            t_new[...] = top
        if mixed is not None:
            r, h = old
            at = pl.ds(pl.multiple_of(h * size, size), size)
            gated = (g_scr[r, at, :] * (acc[:size] / acc[size:size + 1])).astype(jnp.bfloat16)
            left, right = gated[:, :BLOCK], gated[:, BLOCK:]
            g_own[qh * HALF + r, at, :] = jnp.where(qh == 0, left, right)
            g_send[r, at, :] = jnp.where(qh == 0, right, left)
            g_copy(r, h).start()

    def finish(r, carry):
        update = jnp.dot(wot[...], g_own[r], preferred_element_type=jnp.float32).T + oo_ref[...]
        out_ref[r] = update.astype(jnp.bfloat16)
        return carry

    def row_x(k):
        for d in range(3):
            x_copy(k, d).wait_recv()

    def head_z(h):
        for d in range(3):
            b_copy(h, d).wait_recv()
        y_copy(h, 0).start()
        y_copy(h, 2).start()
        pl.when(jnp.logical_not(forwarded(h)))(lambda: y_copy(h, 1).start())

    def head_y(h):
        y_copy(h, 0).wait_recv()
        y_copy(h, 2).wait_recv()

        @pl.when(forwarded(h))
        def _():
            for d in range(2):
                y_forward(h, d).start()

        @pl.when(jnp.logical_not(forwarded(h)))
        def _():
            y_copy(h, 1).wait_recv()
            c_copy(h).start()

    def head_last(h):
        @pl.when(forwarded(h))
        def _():
            for d in range(2):
                y_forward(h, d).wait_recv()
            c_copy(h).start()

    def head_core(h):
        c_copy(h).wait_recv()

    def tile_at(i):
        at = unpacked(TILES, 5, i)
        return at // HEADS, at % HEADS

    def run_part(i):
        at = unpacked(PARTS, 4, i)
        r, d = at // 4, at % 4
        pl.when(d == 0)(lambda: gates(r))
        project(r, (x + d) % 4)

    even, odd = (s_even, t_even), (s_odd, t_odd)

    def run_tile(i):
        new, old = tile_at(i), tile_at(jnp.maximum(i - 1, 0))
        pl.when(i == 0)(lambda: attend(new, *even, None, *odd))
        pl.when(i % 2 == 1)(lambda: attend(new, *odd, old, *even))
        pl.when((i > 0) & (i % 2 == 0))(lambda: attend(new, *even, old, *odd))

    actions = (row_z, row_x, head_z, head_y, head_last, head_core, run_part, run_tile)

    def step(n, counts):
        kind = unpacked(STEPS, 3, n)
        for at, action in enumerate(actions):
            pl.when(kind == at)(lambda action=action, at=at: action(counts[at]))
        return tuple(count + (kind == at).astype(jnp.int32) for at, count in enumerate(counts))

    lax.fori_loop(0, len(STEPS), step, (jnp.int32(0),) * 8)
    last = (TILES[-1] // HEADS, TILES[-1] % HEADS)
    attend(None, *even, last, *odd)
    own_rows = qh * HALF
    lax.fori_loop(own_rows, own_rows + HALF, finish, 0)

    def close_tiles(i, carry):
        g_copy(i // HEADS, i % HEADS).wait_recv()
        return carry

    lax.fori_loop(0, HALF * HEADS, close_tiles, 0)
    lax.fori_loop(HALF - own_rows, 2 * HALF - own_rows, finish, 0)

    def close_rows(k, carry):
        for d in range(3):
            z_copy(k, d).wait_send()
        for d in range(3):
            x_copy(k, d).wait_send()
        for h in range(HEADS):
            g_copy(k, h).wait_send()
        return carry

    def close_heads(h, carry):
        for d in range(3):
            b_copy(h, d).wait_send()
        y_copy(h, 0).wait_send()
        y_copy(h, 2).wait_send()
        pl.when(jnp.logical_not(forwarded(h)))(lambda: y_copy(h, 1).wait_send())

        @pl.when(forwarded(h))
        def _():
            for d in range(2):
                y_forward(h, d).wait_send()

        c_copy(h).wait_send()
        return carry

    lax.fori_loop(0, HEADS, close_heads, 0)
    lax.fori_loop(0, HALF, close_rows, 0)


def body(
    alignment_embedding,
    coupling_embedding,
    asking_projection,
    lookup_projection,
    content_projection,
    filter_projection,
    filter_offset,
    coupling_head_projection,
    final_projection,
    final_offset,
):
    rows, block, depth = alignment_embedding.shape
    heads = coupling_head_projection.shape[1]
    size = depth // heads
    keys = 16 * block
    bf, f32 = jnp.bfloat16, jnp.float32
    sem = pltpu.SemaphoreType.DMA
    vmem = pl.BlockSpec(memory_space=pltpu.VMEM)
    in_specs = [vmem] * 10
    in_specs[1] = pl.BlockSpec(memory_space=pl.ANY)
    return pl.pallas_call(
        fused_kernel,
        out_shape=jax.ShapeDtypeStruct((rows, block, depth), bf),
        in_specs=in_specs,
        out_specs=vmem,
        scratch_shapes=[
            pltpu.VMEM((rows, block, depth), bf),
            pltpu.VMEM((HALF, 4, 4, block, depth), bf),
            pltpu.VMEM((heads, block, block), bf),
            pltpu.VMEM((heads, 2, 4, 2, 2, block, block), bf),
            pltpu.VMEM((block, block, coupling_embedding.shape[2]), bf),
            pltpu.VMEM((block * heads, block), f32),
            pltpu.VMEM((HALF, keys, depth), bf),
            pltpu.VMEM((HALF, heads, size + 16, keys), bf),
            pltpu.VMEM((HALF, depth, 2 * block), bf),
            pltpu.VMEM((HALF, depth, 2 * block), f32),
            pltpu.VMEM((rows, depth, block), bf),
            pltpu.VMEM((HALF, depth, block), bf),
            pltpu.VMEM((keys, 2 * block), f32),
            pltpu.VMEM((keys, 2 * block), f32),
            pltpu.VMEM((8, 2 * block), f32),
            pltpu.VMEM((8, 2 * block), f32),
            pltpu.VMEM((depth, depth), bf),
            pltpu.VMEM((depth, depth), bf),
            pltpu.VMEM((depth, depth), bf),
            pltpu.VMEM((depth, depth), bf),
            pltpu.VMEM((depth, block), f32),
            sem((4,)),
            sem((2,)),
            sem((HALF, 3)),
            sem((HALF, 3)),
            sem((HALF, 4)),
            sem((HALF, 4)),
            sem((heads, 3)),
            sem((heads, 3)),
            sem((heads, 4)),
            sem((heads, 4)),
            sem((heads,)),
            sem((heads,)),
            sem((HALF, heads)),
            sem((HALF, heads)),
        ],
        compiler_params=pltpu.CompilerParams(
            collective_id=0, has_side_effects=True, vmem_limit_bytes=VMEM_LIMIT
        ),
    )(
        alignment_embedding, coupling_embedding, asking_projection, lookup_projection, content_projection,
        filter_projection, filter_offset.reshape(1, depth), coupling_head_projection.T, final_projection,
        final_offset.reshape(1, depth),
    )


def solution(mesh):
    placed = (P("seq", "res", None), P("res", "seq", None), P(), P(), P(), P(), P(), P(), P(), P())
    return jax.shard_map(
        body, mesh=mesh, in_specs=placed, out_specs=P("seq", "res", None), check_vma=False
    )
```

```python
import jax
import jax.numpy as jnp
from jax import lax
from jax.experimental import pallas as pl
from jax.experimental.pallas import tpu as pltpu
from jax.sharding import PartitionSpec as P

MESH = pl.DeviceIdType.MESH
VMEM_LIMIT = 62 * 1024 * 1024
NT = (((1,), (1,)), ((), ()))
HEADS = 8
HALF = 4
BLOCK = 128
STEP = 256
FORWARDED = (2, 6)
STEPS = (
    0, 6, 2, 2, 1, 6, 3, 4, 6, 0, 6, 6, 5, 7, 2, 3, 4, 2, 5, 7, 3, 0, 6, 3, 1,
    6, 6, 4, 6, 7, 2, 7, 5, 7, 4, 7, 2, 5, 7, 7, 3, 0, 6, 3, 1, 6, 6, 6, 7, 4,
    2, 7, 7, 7, 4, 5, 2, 7, 7, 7, 5, 7, 7, 7, 3, 4, 1, 6, 6, 6, 7, 5, 7, 7, 3,
    4, 7, 7, 7, 5, 7, 7, 7, 7, 7, 7, 7, 7,
)
TILES = (
    0, 1, 8, 9, 2, 10, 3, 11, 16, 17, 18, 19, 4, 12, 20, 5,
    13, 21, 24, 25, 26, 27, 28, 29, 6, 14, 22, 30, 7, 15, 23, 31,
)
PARTS = (
    0, 1, 2, 3, 4, 8, 5, 6, 7, 12, 9, 10, 11, 13, 14, 15,
)


def forwarded(h):
    return (h >= FORWARDED[0]) & (h < FORWARDED[1])


def packed(values, bits):
    per = 30 // bits
    return per, [sum(v << (bits * at) for at, v in enumerate(values[i:i + per])) for i in range(0, len(values), per)]


def unpacked(values, bits, index):
    per, words = packed(values, bits)
    word = lookup(words, index // per)
    return (word >> (bits * (index % per))) % (1 << bits)


def lookup(table, index):
    value = jnp.int32(table[0])
    for at in range(1, len(table)):
        value = jnp.where(index >= at, jnp.int32(table[at]), value)
    return value


def standardize_features(x):
    x = x.astype(jnp.float32)
    mean = jnp.mean(x, axis=-1, keepdims=True)
    var = jnp.mean((x - mean) ** 2, axis=-1, keepdims=True)
    return (x - mean) * lax.rsqrt(var + 1e-05)


def fused_kernel(
    m_ref, pair_ref, wq_ref, wk_ref, wv_ref, wf_ref, off_ref, wc_ref, wo_ref, oo_ref,
    out_ref,
    nown, nall, tile, ball, pair_buf, raw, k_scr, v_scr, q_scr, g_scr, g_own, g_send, s_even, s_odd, t_even, t_odd, wqt, wvt, wft, wot, offsets,
    psem, lsem, zs, zr, xs, xr, bs, br, ys, yr, cs, cr, os, orr,
):
    s, res = lax.axis_index("seq"), lax.axis_index("res")
    c, y, zh, x, zl = s % 2, (s // 2) % 4, s // 8, res % 4, res // 4
    qh = zl // 2
    depth = wq_ref.shape[0]
    size = depth // HEADS
    keys = k_scr.shape[1]
    scale = 1.0 / size**0.5

    def device(c_=c, y_=y, zh_=zh, x_=x, zl_=zl):
        return (zh_ * 8 + y_ * 2 + c_, zl_ * 4 + x_)

    z_peers = [device(zl_=(zl + d) % 4) for d in (1, 2, 3)]
    x_peers = [device(x_=(x + d) % 4) for d in (1, 2, 3)]
    y_peers = [device(y_=(y + d) % 4) for d in (1, 2, 3)]
    partner = device(zl_=(zl + 2) % 4)
    b_peers = [partner, device(zh_=1 - zh), device(zh_=1 - zh, zl_=(zl + 2) % 4)]
    sibling = device(c_=1 - c)
    peers = z_peers + x_peers + y_peers + b_peers[1:] + [sibling]

    barrier = pltpu.get_barrier_semaphore()
    for peer in peers:
        pl.semaphore_signal(barrier, inc=1, device_id=peer, device_id_type=MESH)

    chunk = BLOCK // 4

    def pair_copy(i):
        at = pl.ds(i * chunk, chunk)
        return pltpu.make_async_copy(pair_ref.at[at], pair_buf.at[at], psem.at[i])

    for i in range(4):
        pair_copy(i).start()

    def norm_rows(k, carry):
        for i in (k, HALF + k):
            nown[i] = standardize_features(m_ref[i]).astype(jnp.bfloat16)
        return carry

    norm_rows(0, 0)

    def remote(src, dst, send, recv, peer):
        return pltpu.make_async_remote_copy(
            src_ref=src, dst_ref=dst, send_sem=send, recv_sem=recv, device_id=peer, device_id_type=MESH
        )

    def z_copy(k, d):
        to = (zl + d + 1) % 4
        return remote(nown.at[(to // 2) * HALF + k], nall.at[k, x, zl], zs.at[k, d], zr.at[k, d], z_peers[d])

    def x_copy(k, d):
        return remote(nall.at[k, x], nall.at[k, x], xs.at[k, d], xr.at[k, d], x_peers[d])

    def b_copy(h, d):
        return remote(tile.at[h], ball.at[h, c, y, zh, qh], bs.at[h, d], br.at[h, d], b_peers[d])

    def y_copy(h, d):
        return remote(ball.at[h, c, y], ball.at[h, c, y], ys.at[h, d], yr.at[h, d], y_peers[d])

    def y_forward(h, d):
        block = ball.at[h, c, (y + 3) % 4, 0] if d == 0 else ball.at[h, c, (y + 1) % 4, 1]
        return remote(block, block, ys.at[h, 1 + 2 * d], yr.at[h, 1 + 2 * d], y_peers[2 * d])

    def c_copy(h):
        return remote(ball.at[h, c], ball.at[h, c], cs.at[h], cr.at[h], sibling)

    def g_copy(r, h):
        at = pl.ds(pl.multiple_of(h * size, size), size)
        return remote(g_send.at[r, at], g_own.at[qh * HALF + r, at], os.at[r, h], orr.at[r, h], partner)

    own_n = pltpu.make_async_copy(nown.at[pl.ds(qh * HALF, HALF)], nall.at[:, x, zl], lsem.at[0])
    own_b = pltpu.make_async_copy(tile, ball.at[:, c, y, zh, qh], lsem.at[1])

    pl.semaphore_wait(barrier, len(peers))

    def start_z(k):
        for d in range(3):
            z_copy(k, d).start()

    start_z(0)

    wc = wc_ref[...]
    group = 16

    def pair_rows(i, carry):
        at = pl.multiple_of(i * group, group)
        normed = standardize_features(pair_buf[pl.ds(at, group)]).astype(jnp.bfloat16)
        for j in range(group):
            raw[pl.ds(pl.multiple_of((at + j) * HEADS, HEADS), HEADS), :] = lax.dot_general(
                wc, normed[j], NT, preferred_element_type=jnp.float32
            )
        return carry

    def gates(r):
        first = zl % 2
        rows_q = jnp.concatenate([nall[r, x, first], nall[r, x, first + 2]], axis=0)
        q = lax.dot_general(wqt[...], rows_q, NT, preferred_element_type=jnp.float32) * scale
        q_scr[r] = q.astype(jnp.bfloat16)
        gate = lax.dot_general(wft[...], rows_q, NT, preferred_element_type=jnp.float32)
        offset = jnp.concatenate([offsets[...], offsets[...]], axis=1)
        g_scr[r] = jax.nn.sigmoid(gate + offset)

    def project(r, i):
        rows = nall[r, i].reshape(4 * BLOCK, depth)
        at = pl.multiple_of(i * 4 * BLOCK, 4 * BLOCK)
        k_scr[r, pl.ds(at, 4 * BLOCK), :] = jnp.dot(
            rows, wk_ref[...], preferred_element_type=jnp.float32
        ).astype(jnp.bfloat16)
        v = lax.dot_general(wvt[...], rows, NT, preferred_element_type=jnp.float32).astype(jnp.bfloat16)
        for h in range(HEADS):
            v_scr[r, h, pl.ds(0, size), pl.ds(at, 4 * BLOCK)] = v[h * size:(h + 1) * size]

    def row_z(k):
        for d in range(3):
            z_copy(k, d).wait_recv()
        for d in range(3):
            x_copy(k, d).start()

    for i in range(4):
        pair_copy(i).wait()
        lax.fori_loop(i * (chunk // group), (i + 1) * (chunk // group), pair_rows, 0)
    for h in range(HEADS):
        tile[h] = raw[pl.ds(h, BLOCK, stride=HEADS), :].T.astype(jnp.bfloat16)
    own_b.start()

    def start_b(h):
        for d in range(3):
            b_copy(h, d).start()

    start_b(0)
    start_b(1)
    lax.fori_loop(1, HALF, norm_rows, 0)
    own_n.start()
    start_z(1)
    start_b(2)
    start_b(3)
    start_z(2)
    start_b(4)
    start_b(5)
    start_z(3)
    start_b(6)
    start_b(7)
    wqt[...] = wq_ref[...].astype(jnp.float32).T.astype(jnp.bfloat16)
    wvt[...] = wv_ref[...].astype(jnp.float32).T.astype(jnp.bfloat16)
    wft[...] = wf_ref[...].astype(jnp.float32).T.astype(jnp.bfloat16)
    wot[...] = wo_ref[...].astype(jnp.float32).T.astype(jnp.bfloat16)
    offsets[...] = jnp.broadcast_to(off_ref[...], (BLOCK, depth)).T

    own_n.wait()
    own_b.wait()

    def scores(r, h):
        qt = q_scr[r]
        channel = lax.broadcasted_iota(jnp.int32, qt.shape, 0)
        qm = jnp.where((channel >= h * size) & (channel < (h + 1) * size), qt, jnp.zeros_like(qt))

        def block(at, s_ref, top):
            part = jnp.dot(k_scr[r, pl.ds(at, STEP), :], qm, preferred_element_type=jnp.float32)
            biases = []
            for sub in range(at // BLOCK, (at + STEP) // BLOCK):
                j = (sub % 4) * 4 + sub // 4
                here = (h, j % 2, (j // 2) % 4, j // 8)
                biases.append(jnp.concatenate([ball[here + (0,)], ball[here + (1,)]], axis=1))
            part = part + jnp.concatenate(biases, axis=0).astype(jnp.float32)
            s_ref[pl.ds(at, STEP), :] = part
            best = jnp.max(part.reshape(STEP // 8, 8, part.shape[1]), axis=0)
            return best if top is None else jnp.maximum(top, best)

        return block

    def mix(r, h, t_ref):
        top = jnp.max(t_ref[...], axis=0, keepdims=True)

        def block(at, s_ref, acc):
            weights = jnp.exp(s_ref[pl.ds(at, STEP), :] - top)
            total = jnp.sum(weights.reshape(STEP // 8, 8, weights.shape[1]), axis=0)
            part = jnp.dot(
                v_scr[r, h, :, pl.ds(at, STEP)], weights.astype(jnp.bfloat16), preferred_element_type=jnp.float32
            )
            return (part, total) if acc is None else (acc[0] + part, acc[1] + total)

        return block

    def attend(new, s_new, t_new, old, s_old, t_old):
        top = acc = None
        score = None if new is None else scores(*new)
        mixed = None if old is None else mix(*old, t_old)
        for at in range(0, keys, STEP):
            if score is not None:
                top = score(at, s_new, top)
            if mixed is not None:
                acc = mixed(at, s_old, acc)
        if score is not None:
            t_new[...] = top
        if mixed is not None:
            r, h = old
            at = pl.ds(pl.multiple_of(h * size, size), size)
            gated = (g_scr[r, at, :] * (acc[0] / jnp.sum(acc[1], axis=0, keepdims=True))).astype(jnp.bfloat16)
            left, right = gated[:, :BLOCK], gated[:, BLOCK:]
            g_own[qh * HALF + r, at, :] = jnp.where(qh == 0, left, right)
            g_send[r, at, :] = jnp.where(qh == 0, right, left)
            g_copy(r, h).start()

    def finish(r, carry):
        update = jnp.dot(wot[...], g_own[r], preferred_element_type=jnp.float32).T + oo_ref[...]
        out_ref[r] = update.astype(jnp.bfloat16)
        return carry

    def row_x(k):
        for d in range(3):
            x_copy(k, d).wait_recv()

    def head_z(h):
        for d in range(3):
            b_copy(h, d).wait_recv()
        y_copy(h, 0).start()
        y_copy(h, 2).start()
        pl.when(jnp.logical_not(forwarded(h)))(lambda: y_copy(h, 1).start())

    def head_y(h):
        y_copy(h, 0).wait_recv()
        y_copy(h, 2).wait_recv()

        @pl.when(forwarded(h))
        def _():
            for d in range(2):
                y_forward(h, d).start()

        @pl.when(jnp.logical_not(forwarded(h)))
        def _():
            y_copy(h, 1).wait_recv()
            c_copy(h).start()

    def head_last(h):
        @pl.when(forwarded(h))
        def _():
            for d in range(2):
                y_forward(h, d).wait_recv()
            c_copy(h).start()

    def head_core(h):
        c_copy(h).wait_recv()

    def tile_at(i):
        at = unpacked(TILES, 5, i)
        return at // HEADS, at % HEADS

    def run_part(i):
        at = unpacked(PARTS, 4, i)
        r, d = at // 4, at % 4
        pl.when(d == 0)(lambda: gates(r))
        project(r, (x + d) % 4)

    even, odd = (s_even, t_even), (s_odd, t_odd)

    def run_tile(i):
        new, old = tile_at(i), tile_at(jnp.maximum(i - 1, 0))
        pl.when(i == 0)(lambda: attend(new, *even, None, *odd))
        pl.when(i % 2 == 1)(lambda: attend(new, *odd, old, *even))
        pl.when((i > 0) & (i % 2 == 0))(lambda: attend(new, *even, old, *odd))

    actions = (row_z, row_x, head_z, head_y, head_last, head_core, run_part, run_tile)

    def step(n, counts):
        kind = unpacked(STEPS, 3, n)
        for at, action in enumerate(actions):
            pl.when(kind == at)(lambda action=action, at=at: action(counts[at]))
        return tuple(count + (kind == at).astype(jnp.int32) for at, count in enumerate(counts))

    lax.fori_loop(0, len(STEPS), step, (jnp.int32(0),) * 8)
    last = (TILES[-1] // HEADS, TILES[-1] % HEADS)
    attend(None, *even, last, *odd)
    own_rows = qh * HALF
    lax.fori_loop(own_rows, own_rows + HALF, finish, 0)

    def close_tiles(i, carry):
        g_copy(i // HEADS, i % HEADS).wait_recv()
        return carry

    lax.fori_loop(0, HALF * HEADS, close_tiles, 0)
    lax.fori_loop(HALF - own_rows, 2 * HALF - own_rows, finish, 0)

    def close_rows(k, carry):
        for d in range(3):
            z_copy(k, d).wait_send()
        for d in range(3):
            x_copy(k, d).wait_send()
        for h in range(HEADS):
            g_copy(k, h).wait_send()
        return carry

    def close_heads(h, carry):
        for d in range(3):
            b_copy(h, d).wait_send()
        y_copy(h, 0).wait_send()
        y_copy(h, 2).wait_send()
        pl.when(jnp.logical_not(forwarded(h)))(lambda: y_copy(h, 1).wait_send())

        @pl.when(forwarded(h))
        def _():
            for d in range(2):
                y_forward(h, d).wait_send()

        c_copy(h).wait_send()
        return carry

    lax.fori_loop(0, HEADS, close_heads, 0)
    lax.fori_loop(0, HALF, close_rows, 0)


def body(
    alignment_embedding,
    coupling_embedding,
    asking_projection,
    lookup_projection,
    content_projection,
    filter_projection,
    filter_offset,
    coupling_head_projection,
    final_projection,
    final_offset,
):
    rows, block, depth = alignment_embedding.shape
    heads = coupling_head_projection.shape[1]
    size = depth // heads
    keys = 16 * block
    bf, f32 = jnp.bfloat16, jnp.float32
    sem = pltpu.SemaphoreType.DMA
    vmem = pl.BlockSpec(memory_space=pltpu.VMEM)
    in_specs = [vmem] * 10
    in_specs[1] = pl.BlockSpec(memory_space=pl.ANY)
    return pl.pallas_call(
        fused_kernel,
        out_shape=jax.ShapeDtypeStruct((rows, block, depth), bf),
        in_specs=in_specs,
        out_specs=vmem,
        scratch_shapes=[
            pltpu.VMEM((rows, block, depth), bf),
            pltpu.VMEM((HALF, 4, 4, block, depth), bf),
            pltpu.VMEM((heads, block, block), bf),
            pltpu.VMEM((heads, 2, 4, 2, 2, block, block), bf),
            pltpu.VMEM((block, block, coupling_embedding.shape[2]), bf),
            pltpu.VMEM((block * heads, block), f32),
            pltpu.VMEM((HALF, keys, depth), bf),
            pltpu.VMEM((HALF, heads, size, keys), bf),
            pltpu.VMEM((HALF, depth, 2 * block), bf),
            pltpu.VMEM((HALF, depth, 2 * block), f32),
            pltpu.VMEM((rows, depth, block), bf),
            pltpu.VMEM((HALF, depth, block), bf),
            pltpu.VMEM((keys, 2 * block), f32),
            pltpu.VMEM((keys, 2 * block), f32),
            pltpu.VMEM((8, 2 * block), f32),
            pltpu.VMEM((8, 2 * block), f32),
            pltpu.VMEM((depth, depth), bf),
            pltpu.VMEM((depth, depth), bf),
            pltpu.VMEM((depth, depth), bf),
            pltpu.VMEM((depth, depth), bf),
            pltpu.VMEM((depth, block), f32),
            sem((4,)),
            sem((2,)),
            sem((HALF, 3)),
            sem((HALF, 3)),
            sem((HALF, 4)),
            sem((HALF, 4)),
            sem((heads, 3)),
            sem((heads, 3)),
            sem((heads, 4)),
            sem((heads, 4)),
            sem((heads,)),
            sem((heads,)),
            sem((HALF, heads)),
            sem((HALF, heads)),
        ],
        compiler_params=pltpu.CompilerParams(
            collective_id=0, has_side_effects=True, vmem_limit_bytes=VMEM_LIMIT
        ),
    )(
        alignment_embedding, coupling_embedding, asking_projection, lookup_projection, content_projection,
        filter_projection, filter_offset.reshape(1, depth), coupling_head_projection.T, final_projection,
        final_offset.reshape(1, depth),
    )


def solution(mesh):
    placed = (P("seq", "res", None), P("res", "seq", None), P(), P(), P(), P(), P(), P(), P(), P())
    return jax.shard_map(
        body, mesh=mesh, in_specs=placed, out_specs=P("seq", "res", None), check_vma=False
    )
```
